256 devices in a mesh: dp: 16 (over z_lo, x), context: 16 (over z_hi, y, core).
Axes of the slice: x: 4, y: 4, z: 8 (z_hi: 2, z_lo: 4; z = z_hi * 4 + z_lo), core: 2. Of those that a mesh axis runs over, the one named last changes fastest.
Arguments:
- queries: bfloat16 [16, 2048, 4096], P('dp', 'context'), may hold values from -8 to 8
- keys_values: bfloat16 [16, 2048, 2, 512], P('dp', 'context'), may hold values from -8 to 8
- key_tangents: bfloat16 [16, 2048, 2, 512], P('dp', 'context'), may hold values from -20 to 20
- output_adjoint_rows: bfloat16 [16, 2048, 4096], P('dp', 'context'), may hold values from -0.59765625 to 0.59765625
- segments: int32 [16, 2048], P('dp'), may hold values from 0 to 3, as said below
- span_pair: int32 [16], replicated, may hold values from 0 to 15, as said below
Outputs:
- hess_queries: bfloat16 [16, 2048, 4096], P('dp', 'context')
- hess_keys_values: bfloat16 [16, 2048, 2, 512], P('dp', 'context')
- curvature: float32 [], replicated
The draws below stay inside these ranges and needn't reach their ends.
Inputs may be any that keep to these rules, and one draw needn't show every extreme that they name: `span_pair`: A permutation of 0 to 15. `segments`: ids never fall along positions within a window, start at 0, and every window holds exactly four documents.
All inputs are finite; a program needn't handle non-finite values.
Results may differ from the reference program's by a relative error of at most 0.03.
Values may be sent and summed in bfloat16 or wider, within the bound.
A program may use at most 256 MiB of HBM per device.

```python
import jax
import jax.numpy as jnp
from jax import lax

HEAD_SIZE = 128
QUERY_HEADS = 32
KEY_VALUE_HEADS = 4
TOK_DEV = 128
WINDOW_LENGTH = 2048
PACKED_WINDOWS = 16


def span_order(key):
    return jax.random.permutation(jax.random.fold_in(key, 11), WINDOW_LENGTH // TOK_DEV).astype(jnp.int32)


def stored_positions(pair):
    span = TOK_DEV // 2
    token_count = WINDOW_LENGTH // TOK_DEV
    rows = jnp.arange(WINDOW_LENGTH, dtype=jnp.int32)
    device = rows // TOK_DEV
    within = rows % TOK_DEV
    table = jnp.arange(token_count, dtype=jnp.int32)
    first = jnp.sum(jnp.where(device[:, None] == table[None, :], pair[None, :], 0), axis=1).astype(jnp.int32)
    block = jnp.where(within // span == 0, first, 2 * token_count - 1 - first)
    return (block * span + within % span).astype(jnp.int32)


def draw_queries(key, part):
    key = jax.random.fold_in(key, 1)
    array_shape = (PACKED_WINDOWS, WINDOW_LENGTH, QUERY_HEADS * HEAD_SIZE)
    base = jax.random.truncated_normal(key, -6.0, 6.0, array_shape, jnp.float32)
    return base.astype(jnp.bfloat16)


def draw_keys_values(key, part):
    key = jax.random.fold_in(key, 2)
    array_shape = (PACKED_WINDOWS, WINDOW_LENGTH, 2, KEY_VALUE_HEADS * HEAD_SIZE)
    base = jax.random.truncated_normal(key, -6.0, 6.0, array_shape, jnp.float32)
    return base.astype(jnp.bfloat16)


def draw_key_tangents(key, part):
    key = jax.random.fold_in(key, 3)
    array_shape = (PACKED_WINDOWS, WINDOW_LENGTH, 2, KEY_VALUE_HEADS * HEAD_SIZE)
    rows = jnp.arange(WINDOW_LENGTH, dtype=jnp.float32)
    windows = jnp.arange(PACKED_WINDOWS, dtype=jnp.float32)
    rise = (1.0 + 2.0 * rows / max(WINDOW_LENGTH - 1, 1))[None, :, None, None] * (1.0 + 2.0 * windows / max(PACKED_WINDOWS - 1, 1))[:, None, None, None]
    base = jax.random.truncated_normal(key, -6.0, 6.0, array_shape, jnp.float32)
    return (0.3 * base * rise).astype(jnp.bfloat16)


def draw_segments(key, part):
    pair = span_order(key)
    key = jax.random.fold_in(key, 4)
    window_keys = jax.random.split(key, PACKED_WINDOWS)
    bounds = jax.vmap(lambda one: jax.random.permutation(one, WINDOW_LENGTH - 1)[:3] + 1)(window_keys).astype(jnp.int32)
    rows = jnp.arange(WINDOW_LENGTH, dtype=jnp.int32)
    natural = jnp.sum((rows[None, :, None] >= bounds[:, None, :]).astype(jnp.int32), axis=2).astype(jnp.int32)
    return natural[:, stored_positions(pair)]


def draw_span_pair(key, part):
    return span_order(key)


def level_of(key, shape, cuts, least, largest):
    def one(dim, shards_of):
        steps = jax.random.uniform(jax.random.fold_in(jax.random.fold_in(key, 6), dim), (shards_of,), jnp.float32, least / len(cuts), largest / len(cuts))
        return jnp.repeat(jnp.exp(steps), shape[dim] // shards_of).reshape((-1,) + (1,) * (len(shape) - dim - 1))

    level = one(*cuts[0])
    for cut in cuts[1:]:
        level = level * one(*cut)
    return level


def noise(key, dims, scale, most, cuts=(), kind=jnp.bfloat16):
    array = scale * jax.random.normal(key, dims, jnp.float32)
    if cuts:
        array = array * level_of(key, dims, cuts, -0.22, 0.18)
    return jnp.clip(array, -most, most).astype(kind)


def setup_inputs(seed: int = 0) -> dict:
    splits = jax.random.split(jax.random.key(seed), 7)
    queries = draw_queries(jax.random.fold_in(splits[6], 71), 0)
    keys_values = draw_keys_values(jax.random.fold_in(splits[6], 71), 0)
    key_tangents = draw_key_tangents(jax.random.fold_in(splits[6], 71), 0)
    output_adjoint_rows = noise(splits[3], (PACKED_WINDOWS, WINDOW_LENGTH, QUERY_HEADS * HEAD_SIZE), 0.1, 0.59765625, ((0, 16), (1, 16)))
    segments = draw_segments(jax.random.fold_in(splits[6], 71), 0)
    span_pair = draw_span_pair(jax.random.fold_in(splits[6], 71), 0)
    return {"queries": queries, "keys_values": keys_values, "key_tangents": key_tangents, "output_adjoint_rows": output_adjoint_rows, "segments": segments, "span_pair": span_pair}


def positions(rows, pair, tok_dev):
    span = tok_dev // 2
    token_count = pair.shape[0]
    device = rows // tok_dev
    within = rows % tok_dev
    table = jnp.arange(token_count, dtype=jnp.int32)
    first = jnp.sum(jnp.where(device[:, None] == table[None, :], pair[None, :], 0), axis=1).astype(jnp.int32)
    block = jnp.where(within // span == 0, first, 2 * token_count - 1 - first)
    return (block * span + within % span).astype(jnp.int32)


def head_group(query_matrix, key_matrix, value_matrix, key_direction, value_direction, output_adjoint, seen, scale):
    query_matrix = query_matrix.astype(jnp.float32)
    output_adjoint = output_adjoint.astype(jnp.float32)
    key_matrix = key_matrix.astype(jnp.float32)
    value_matrix = value_matrix.astype(jnp.float32)
    key_direction = key_direction.astype(jnp.float32)
    value_direction = value_direction.astype(jnp.float32)
    logits = scale * jnp.einsum("tgd,sd->gts", query_matrix, key_matrix)
    masked = jnp.where(seen[None], logits, jnp.float32(-1e30))
    peak = jnp.max(masked, axis=-1, keepdims=True)
    weight = jnp.where(seen[None], jnp.exp(masked - peak), jnp.float32(0.0))
    prob = weight / jnp.sum(weight, axis=-1, keepdims=True)
    dprob = jnp.einsum("tgd,sd->gts", output_adjoint, value_matrix)
    tlogits = scale * jnp.einsum("tgd,sd->gts", query_matrix, key_direction)
    tdprob = jnp.einsum("tgd,sd->gts", output_adjoint, value_direction)
    mean_t = jnp.sum(prob * tlogits, axis=-1, keepdims=True)
    delta = jnp.sum(prob * dprob, axis=-1, keepdims=True)
    extra = jnp.sum(prob * tlogits * dprob, axis=-1, keepdims=True)
    tail = jnp.sum(prob * tdprob, axis=-1, keepdims=True)
    tprob = prob * (tlogits - mean_t)
    dscore = prob * (dprob - delta)
    tdelta = extra - mean_t * delta + tail
    tdscore = tprob * (dprob - delta) + prob * (tdprob - tdelta)
    dscore_b = dscore.astype(jnp.bfloat16).astype(jnp.float32)
    tdscore_b = tdscore.astype(jnp.bfloat16).astype(jnp.float32)
    tprob_b = tprob.astype(jnp.bfloat16).astype(jnp.float32)
    hess_q = scale * (jnp.einsum("gts,sd->tgd", tdscore_b, key_matrix) + jnp.einsum("gts,sd->tgd", dscore_b, key_direction))
    hessian_key = scale * jnp.einsum("gts,tgd->sd", tdscore_b, query_matrix)
    hessian_value = jnp.einsum("gts,tgd->sd", tprob_b, output_adjoint)
    return hess_q, hessian_key, hessian_value


def reference(queries, keys_values, key_tangents, output_adjoint_rows, segments, span_pair):
    query_group = QUERY_HEADS // KEY_VALUE_HEADS
    scale = float(HEAD_SIZE) ** -0.5
    rows = jnp.arange(WINDOW_LENGTH, dtype=jnp.int32)
    pos = positions(rows, span_pair, TOK_DEV)
    causal = pos[None, :] <= pos[:, None]

    def window(items):
        query_matrix, key_value_couple, tangent_couple, output_adjoint, seg = items
        seen = causal & (seg[None, :] == seg[:, None])
        query_matrix = query_matrix.reshape(WINDOW_LENGTH, KEY_VALUE_HEADS, query_group, HEAD_SIZE)
        output_adjoint = output_adjoint.reshape(WINDOW_LENGTH, KEY_VALUE_HEADS, query_group, HEAD_SIZE)
        key_matrix = key_value_couple[:, 0].reshape(WINDOW_LENGTH, KEY_VALUE_HEADS, HEAD_SIZE)
        value_matrix = key_value_couple[:, 1].reshape(WINDOW_LENGTH, KEY_VALUE_HEADS, HEAD_SIZE)
        key_direction = tangent_couple[:, 0].reshape(WINDOW_LENGTH, KEY_VALUE_HEADS, HEAD_SIZE)
        value_direction = tangent_couple[:, 1].reshape(WINDOW_LENGTH, KEY_VALUE_HEADS, HEAD_SIZE)
        q_parts, key_portions, value_portions = [], [], []
        for head_number in range(KEY_VALUE_HEADS):
            hq, hk, hv = head_group(query_matrix[:, head_number], key_matrix[:, head_number], value_matrix[:, head_number], key_direction[:, head_number], value_direction[:, head_number], output_adjoint[:, head_number], seen, scale)
            q_parts.append(hq)
            key_portions.append(hk)
            value_portions.append(hv)
        hess_q = jnp.stack(q_parts, axis=1).reshape(WINDOW_LENGTH, QUERY_HEADS * HEAD_SIZE).astype(jnp.bfloat16)
        hessian_key = jnp.stack(key_portions, axis=1).reshape(WINDOW_LENGTH, KEY_VALUE_HEADS * HEAD_SIZE)
        hessian_value = jnp.stack(value_portions, axis=1).reshape(WINDOW_LENGTH, KEY_VALUE_HEADS * HEAD_SIZE)
        return hess_q, jnp.stack([hessian_key, hessian_value], axis=1)

    hess_queries, key_hessian = lax.map(window, (queries, keys_values, key_tangents, output_adjoint_rows, segments))
    curvature = jnp.sum(key_tangents.astype(jnp.float32) * key_hessian) / (PACKED_WINDOWS * WINDOW_LENGTH)
    return hess_queries, key_hessian.astype(jnp.bfloat16), curvature
```

```python
import functools

import jax
import jax.numpy as jnp
from jax import lax
from jax.experimental import pallas as pl
from jax.experimental.pallas import tpu as pltpu
from jax.sharding import PartitionSpec as P

HEAD = 128
QUERY_HEADS = 32
KV_HEADS = 4
TOK = 128
SPAN = 64
WINDOW = 2048
SHARDS = 16
HALF = 8
OWN_HEADS = 4
OWN_COLS = OWN_HEADS * HEAD
ROWS = OWN_HEADS * SPAN
TILE = 128
TILES = WINDOW // TILE
BLOCKS = WINDOW // SPAN
SCALE = float(HEAD) ** -0.5
LOG2E = 1.4426950408889634
EXP_SCALE = SCALE * LOG2E
SAFE_LOG2 = 60.0
MESH = pl.DeviceIdType.MESH
F32 = jnp.float32
BF16 = jnp.bfloat16


def coordinates():
    dp = lax.axis_index("dp")
    context = lax.axis_index("context")
    return dp, context // HALF, (context // 2) % 4, context % 2


def context_index(z_hi, y, core):
    return z_hi * HALF + y * 2 + core


def remote(src, dst, send, recv, device):
    return pltpu.make_async_remote_copy(
        src_ref=src, dst_ref=dst, send_sem=send, recv_sem=recv, device_id=device, device_id_type=MESH
    )


def enter(devices):
    barrier = pltpu.get_barrier_semaphore()
    for device in devices:
        pl.semaphore_signal(barrier, inc=1, device_id=device, device_id_type=MESH)
    pl.semaphore_wait(barrier, len(devices))


def columns_of(y, core):
    return pl.ds(pl.multiple_of((y * 2 + core) * OWN_COLS, OWN_COLS), OWN_COLS)


def spread_kernel(q, g, kv, q_out, g_out, kv_out, kv_send, sib_send, z_send, zsib_send, q_send, g_send, kv_recv, q_recv, g_recv, local):
    dp, zh, y, c = coordinates()
    me = context_index(zh, y, c)
    sibling = (dp, context_index(zh, y, 1 - c))
    across = (dp, context_index(1 - zh, y, c))
    peers = []
    for dy in (1, 3, 2, 0):
        for dc in (0, 1):
            if dy or dc:
                peers.append(((y + dy) % 4, (c + dc) % 2))
    enter([(dp, context_index(zh, py, pc)) for py, pc in peers] + [across])

    own = zh * HALF + y * 2 + c
    slot_here = y * 2 + c
    locals_ = [
        pltpu.make_async_copy(kv.at[y], kv_out.at[own], local.at[0]),
        pltpu.make_async_copy(q.at[:, columns_of(y, c)], q_out.at[slot_here], local.at[1]),
        pltpu.make_async_copy(g.at[:, columns_of(y, c)], g_out.at[slot_here], local.at[2]),
    ]
    copies = []

    def start(copy):
        copy.start()
        copies.append(copy)

    for n, dy in enumerate((1, 3, 2)):
        ty = (y + dy) % 4
        start(remote(kv.at[ty], kv_out.at[own], kv_send.at[n], kv_recv.at[own], (dp, context_index(zh, ty, c))))
    start(remote(kv.at[y], kv_out.at[own], z_send.at[0], kv_recv.at[own], across))
    start(remote(kv.at[y], kv_out.at[own], sib_send.at[0], kv_recv.at[own], sibling))
    for copy in locals_:
        copy.start()
    for n, dy in enumerate((1, 3, 2)):
        slot = context_index(zh, (y + 4 - dy) % 4, c)
        here = kv_out.at[slot]
        remote(here, here, kv_send.at[n], kv_recv.at[slot], across).wait_recv()
        start(remote(here, here, z_send.at[1 + n], kv_recv.at[slot], across))
        start(remote(here, here, sib_send.at[1 + n], kv_recv.at[slot], sibling))
    for n, (py, pc) in enumerate(peers):
        target = (dp, context_index(zh, py, pc))
        start(remote(q.at[:, columns_of(py, pc)], q_out.at[slot_here], q_send.at[n], q_recv.at[slot_here], target))
        start(remote(g.at[:, columns_of(py, pc)], g_out.at[slot_here], g_send.at[n], g_recv.at[slot_here], target))
    for n, dy in enumerate((0, 1, 3, 2)):
        slot = context_index(1 - zh, (y + 4 - dy) % 4, c)
        here = kv_out.at[slot]
        remote(here, here, z_send.at[n], kv_recv.at[slot], across).wait_recv()
        start(remote(here, here, zsib_send.at[n], kv_recv.at[slot], sibling))
    for z in range(2):
        for ys in range(4):
            slot = context_index(z, ys, 1 - c)
            here = kv_out.at[slot]
            remote(here, here, z_send.at[0], kv_recv.at[slot], sibling).wait_recv()
    for n, (py, pc) in enumerate(peers):
        slot = py * 2 + pc
        remote(q_out.at[slot], q_out.at[slot], q_send.at[n], q_recv.at[slot], sibling).wait_recv()
        remote(g_out.at[slot], g_out.at[slot], g_send.at[n], g_recv.at[slot], sibling).wait_recv()
    for copy in copies:
        copy.wait_send()
    for copy in locals_:
        copy.wait()


def spread(q, g, kv):
    any_ = pl.BlockSpec(memory_space=pl.ANY)
    dma = pltpu.SemaphoreType.DMA
    return pl.pallas_call(
        spread_kernel,
        out_shape=(
            jax.ShapeDtypeStruct((HALF, TOK, OWN_COLS), BF16),
            jax.ShapeDtypeStruct((HALF, TOK, OWN_COLS), BF16),
            jax.ShapeDtypeStruct((SHARDS, 4, TOK, HEAD), BF16),
        ),
        in_specs=[any_] * 3,
        out_specs=(any_,) * 3,
        scratch_shapes=[
            dma((3,)), dma((4,)), dma((4,)), dma((4,)), dma((7,)), dma((7,)),
            dma((SHARDS,)), dma((HALF,)), dma((HALF,)), dma((3,)),
        ],
        compiler_params=pltpu.CompilerParams(collective_id=0, has_side_effects=True),
        name="spread",
    )(q, g, kv)


def nt_dot(a, b):
    return lax.dot_general(a, b, (((1,), (1,)), ((), ())), preferred_element_type=F32)


def nn_dot(a, b):
    return jnp.dot(a, b, preferred_element_type=F32)


def fold_rows(x):
    return jnp.sum(x.reshape(x.shape[0] // 8, 8, x.shape[1]), axis=0)


def hvp_kernel(pair, seg, q, g, kv, hq_out, hkv_out, curv_out, kt, vt, kt_t, hk_acc, hv_acc, hq_acc):
    _, zh, _, _ = coordinates()
    segments = seg[...]
    starts = [jnp.sum((segments < d).astype(jnp.int32)) for d in (1, 2, 3)]

    ones = jnp.ones((HEAD, HEAD), BF16)

    def prepare(i, carry):
        first = pair[i]
        for half in range(2):
            block = first if half == 0 else BLOCKS - 1 - first
            tile = block // (TILE // SPAN)
            off = pl.multiple_of((block % (TILE // SPAN)) * SPAN, SPAN)
            rows = pl.ds(half * SPAN, SPAN)
            k = kv[i, 0, rows, :]
            kt[tile, pl.ds(off, SPAN), :] = k
            kt[tile, pl.ds(off + TILE, SPAN), :] = kv[i, 2, rows, :]
            vt[tile, pl.ds(off, SPAN), :] = kv[i, 1, rows, :]
            vt[tile, pl.ds(off + TILE, SPAN), :] = kv[i, 3, rows, :]
            k32 = k.astype(F32)
            carry = jnp.maximum(carry, fold_max(nn_dot((k32 * k32).astype(BF16), ones)))
        return carry

    def fold_max(x):
        return jnp.max(x.reshape(x.shape[0] // 8, 8, x.shape[1]), axis=0)

    key_norm = lax.fori_loop(0, SHARDS, prepare, jnp.zeros((8, HEAD), F32))

    def transpose_tile(t, carry):
        both = kt[t].astype(F32)
        kt_t[t, :, 0:TILE] = both[:TILE].T.astype(BF16)
        kt_t[t, :, TILE:] = both[TILE:].T.astype(BF16)
        hk_acc[t] = jnp.zeros((TILE, HEAD), F32)
        hv_acc[t] = jnp.zeros((TILE, HEAD), F32)
        return carry

    lax.fori_loop(0, TILES, transpose_tile, 0)

    def query_norms(s, carry):
        for h in range(OWN_HEADS):
            x = q[s, :, h * HEAD:(h + 1) * HEAD].astype(F32)
            carry = jnp.maximum(carry, fold_max(nn_dot((x * x).astype(BF16), ones)))
        return carry

    query_norm = lax.fori_loop(0, HALF, query_norms, jnp.zeros((8, HEAD), F32))
    bound = jnp.max(key_norm) * jnp.max(query_norm) * (EXP_SCALE * EXP_SCALE)
    safe = bound < SAFE_LOG2 * SAFE_LOG2

    lane = lax.broadcasted_iota(jnp.int32, (1, ROWS), 1)
    key_row = lax.broadcasted_iota(jnp.int32, (TILE, 1), 0)

    def query_block(n, carry):
        s = n // 2
        half = n % 2
        first = pair[zh * HALF + s]
        block = jnp.where(half == 0, first, BLOCKS - 1 - first)
        base = block * SPAN
        rows = pl.ds(pl.multiple_of(half * SPAN, SPAN), SPAN)
        qb = jnp.concatenate([q[s, rows, h * HEAD:(h + 1) * HEAD] for h in range(OWN_HEADS)], axis=0)
        gb = jnp.concatenate([g[s, rows, h * HEAD:(h + 1) * HEAD] for h in range(OWN_HEADS)], axis=0)
        query_pos = base + lane % SPAN
        doc_start = jnp.zeros_like(query_pos)
        low = jnp.int32(0)
        for start in starts:
            doc_start = jnp.where(query_pos >= start, start, doc_start)
            low = jnp.where(base >= start, start, low)
        first_tile = low // TILE
        last_tile = base // TILE + 1

        def seen_in(t):
            key_pos = t * TILE + key_row
            return (key_pos >= doc_start) & (key_pos <= query_pos)

        def peak_pass(_):
            def step(t, top):
                logits = nt_dot(kt[t, :TILE], qb) * EXP_SCALE
                masked = jnp.where(seen_in(t), logits, -1e30)
                return jnp.maximum(top, fold_max(masked))
            top = lax.fori_loop(first_tile, last_tile, step, jnp.full((8, ROWS), -1e30, F32))
            return jnp.max(top, axis=0, keepdims=True)

        peak = lax.cond(safe, lambda _: jnp.zeros((1, ROWS), F32), peak_pass, 0)

        def stats_step(t, carry):
            total, mu, delta, mixed = carry
            st = nt_dot(kt[t], qb)
            dt = nt_dot(vt[t], gb)
            w = jnp.where(seen_in(t), jnp.exp2(st[:TILE] * EXP_SCALE - peak), 0.0)
            ts = st[TILE:] * SCALE
            dprob = dt[:TILE]
            total = total + fold_rows(w)
            mu = mu + fold_rows(w * ts)
            delta = delta + fold_rows(w * dprob)
            mixed = mixed + fold_rows(w * (ts * dprob + dt[TILE:]))
            return total, mu, delta, mixed

        zero = jnp.zeros((8, ROWS), F32)
        sums = lax.fori_loop(first_tile, last_tile, stats_step, (zero,) * 4)
        total, mu, delta, mixed = [jnp.sum(x, axis=0, keepdims=True) for x in sums]
        inverse = 1.0 / total
        mu = mu * inverse
        delta = delta * inverse
        tdelta = mixed * inverse - mu * delta
        level = peak + jnp.log2(total)

        hq_acc[...] = jnp.zeros_like(hq_acc)

        def grads_step(t, carry):
            st = nt_dot(kt[t], qb)
            dt = nt_dot(vt[t], gb)
            prob = jnp.where(seen_in(t), jnp.exp2(st[:TILE] * EXP_SCALE - level), 0.0)
            tsc = st[TILE:] * SCALE - mu
            dpc = dt[:TILE] - delta
            tdc = dt[TILE:] - tdelta
            tp = (prob * tsc).astype(BF16)
            ds = (prob * dpc).astype(BF16)
            tds = (prob * (tsc * dpc + tdc)).astype(BF16)
            hk_acc[t] += nn_dot(tds, qb)
            hv_acc[t] += nn_dot(tp, gb)
            hq_acc[...] += nn_dot(kt_t[t], jnp.concatenate([tds, ds], axis=0))
            return carry

        lax.fori_loop(first_tile, last_tile, grads_step, 0)
        hq = (hq_acc[...] * SCALE).T.astype(BF16)
        for h in range(OWN_HEADS):
            hq_out[s, rows, h * HEAD:(h + 1) * HEAD] = hq[h * SPAN:(h + 1) * SPAN]
        return carry

    lax.fori_loop(0, 2 * HALF, query_block, 0)

    def finish(i, carry):
        first = pair[i]
        for half in range(2):
            block = first if half == 0 else BLOCKS - 1 - first
            tile = block // (TILE // SPAN)
            off = pl.multiple_of((block % (TILE // SPAN)) * SPAN, SPAN)
            rows = pl.ds(half * SPAN, SPAN)
            hk = hk_acc[tile, pl.ds(off, SPAN), :] * SCALE
            hv = hv_acc[tile, pl.ds(off, SPAN), :]
            carry = carry + fold_rows(kv[i, 2, rows, :].astype(F32) * hk)
            carry = carry + fold_rows(kv[i, 3, rows, :].astype(F32) * hv)
            z = i // HALF
            ys = (i // 2) % 4
            core = i % 2
            hkv_out[core, z, ys, 0, rows, :] = hk.astype(BF16)
            hkv_out[core, z, ys, 1, rows, :] = hv.astype(BF16)
        return carry

    curv = lax.fori_loop(0, SHARDS, finish, jnp.zeros((8, HEAD), F32))
    curv_out[...] = jnp.full((8, HEAD), jnp.sum(curv), F32)


def hvp(pair, seg, q, g, kv):
    vmem = pl.BlockSpec(memory_space=pltpu.VMEM)
    return pl.pallas_call(
        hvp_kernel,
        out_shape=(
            jax.ShapeDtypeStruct((HALF, TOK, OWN_COLS), BF16),
            jax.ShapeDtypeStruct((2, 2, 4, 2, TOK, HEAD), BF16),
            jax.ShapeDtypeStruct((8, HEAD), F32),
        ),
        in_specs=[pl.BlockSpec(memory_space=pltpu.SMEM)] + [vmem] * 4,
        out_specs=(vmem,) * 3,
        scratch_shapes=[
            pltpu.VMEM((TILES, 2 * TILE, HEAD), BF16),
            pltpu.VMEM((TILES, 2 * TILE, HEAD), BF16),
            pltpu.VMEM((TILES, HEAD, 2 * TILE), BF16),
            pltpu.VMEM((TILES, TILE, HEAD), F32),
            pltpu.VMEM((TILES, TILE, HEAD), F32),
            pltpu.VMEM((HEAD, ROWS), F32),
        ],
        compiler_params=pltpu.CompilerParams(vmem_limit_bytes=50 << 20),
        name="hvp",
    )(pair, seg, q, g, kv)


def collect_kernel(hq, hkv, curv, hq_out, hkv_out, curv_out, sib_buf, z_buf, z_stage, y_stage, a_buf, b_buf, c_buf, b_own, c_own, hq_send, hq_recv, sib_send, sib_recv, z_send, z_recv, y_send, y_recv, a_send, a_recv, b_send, b_recv, c_send, c_recv, local):
    dp, zh, y, c = coordinates()
    x = dp % 4
    z_lo = dp // 4
    z = zh * 4 + z_lo
    sibling = (dp, context_index(zh, y, 1 - c))
    across = (dp, context_index(1 - zh, y, c))
    peers = []
    for dy in (1, 3, 2, 0):
        for dc in (0, 1):
            if dy or dc:
                peers.append(((y + dy) % 4, (c + dc) % 2))
    row_devices = [(dp, context_index(zh, py, pc)) for py, pc in peers]
    z_peers = [(z + dz) % 8 for dz in range(1, 8)]
    z_devices = [((pz % 4) * 4 + x, context_index(pz // 4, y, c)) for pz in z_peers]
    x_peers = [(x + dx) % 4 for dx in range(1, 4)]
    x_devices = [(z_lo * 4 + px, context_index(zh, y, c)) for px in x_peers]
    enter(row_devices + z_devices + x_devices)

    copies = []

    def start(copy):
        copy.start()
        copies.append(copy)

    slot_here = y * 2 + c
    for n, which in enumerate((1 - zh, zh)):
        start(remote(hkv.at[1 - c, which], sib_buf.at[which], sib_send.at[n], sib_recv.at[n], sibling))
    for n, device in enumerate(row_devices):
        start(remote(curv, a_buf.at[slot_here], a_send.at[n], a_recv.at[slot_here], device))
    for n, (py, pc) in enumerate(peers):
        start(remote(hq.at[py * 2 + pc], hq_out.at[:, columns_of(y, c)], hq_send.at[n], hq_recv.at[slot_here], row_devices[n]))
    own_hq = pltpu.make_async_copy(hq.at[slot_here], hq_out.at[:, columns_of(y, c)], local.at[0])
    own_hq.start()

    other = 1 - zh
    remote(sib_buf.at[other], sib_buf.at[other], sib_send.at[0], sib_recv.at[0], sibling).wait_recv()
    for ys in range(4):
        for part in range(2):
            z_stage[ys, part] = (hkv[c, other, ys, part].astype(F32) + sib_buf[other, ys, part].astype(F32)).astype(BF16)
    start(remote(z_stage, z_buf, z_send, z_recv, across))

    for n, (py, pc) in enumerate(peers):
        slot = py * 2 + pc
        remote(a_buf.at[slot], a_buf.at[slot], a_send.at[n], a_recv.at[slot], sibling).wait_recv()
    a_buf[slot_here] = curv[...]
    b_own[...] = jnp.sum(a_buf[...], axis=0)
    for n, device in enumerate(z_devices):
        start(remote(b_own, b_buf.at[z], b_send.at[n], b_recv.at[z], device))
    for n, pz in enumerate(z_peers):
        remote(b_buf.at[pz], b_buf.at[pz], b_send.at[n], b_recv.at[pz], sibling).wait_recv()
    b_buf[z] = b_own[...]
    c_own[...] = jnp.sum(b_buf[...], axis=0)
    for n, device in enumerate(x_devices):
        start(remote(c_own, c_buf.at[x], c_send.at[n], c_recv.at[x], device))
    for n, px in enumerate(x_peers):
        remote(c_buf.at[px], c_buf.at[px], c_send.at[n], c_recv.at[px], sibling).wait_recv()
    c_buf[x] = c_own[...]
    curv_out[...] = jnp.sum(c_buf[...], axis=0) * (1.0 / (SHARDS * WINDOW))

    remote(sib_buf.at[zh], sib_buf.at[zh], sib_send.at[1], sib_recv.at[1], sibling).wait_recv()
    remote(z_stage, z_buf, z_send, z_recv, across).wait_recv()
    for ys in range(4):
        for part in range(2):
            total = hkv[c, zh, ys, part].astype(F32) + sib_buf[zh, ys, part].astype(F32) + z_buf[ys, part].astype(F32)
            y_stage[ys, part] = total.astype(BF16)
    for n, dy in enumerate((1, 3, 2)):
        ty = (y + dy) % 4
        start(remote(y_stage.at[ty], hkv_out.at[y], y_send.at[n], y_recv.at[y], (dp, context_index(zh, ty, c))))
    own_kv = pltpu.make_async_copy(y_stage.at[y], hkv_out.at[y], local.at[1])
    own_kv.start()
    for n, dy in enumerate((1, 3, 2)):
        ty = (y + dy) % 4
        remote(hkv_out.at[ty], hkv_out.at[ty], y_send.at[n], y_recv.at[ty], sibling).wait_recv()
    for n, (py, pc) in enumerate(peers):
        slot = py * 2 + pc
        remote(hq.at[slot], hq_out.at[:, columns_of(py, pc)], hq_send.at[n], hq_recv.at[slot], sibling).wait_recv()
    for copy in copies:
        copy.wait_send()
    own_hq.wait()
    own_kv.wait()


def collect(hq, hkv, curv):
    vmem = pl.BlockSpec(memory_space=pltpu.VMEM)
    any_ = pl.BlockSpec(memory_space=pl.ANY)
    dma = pltpu.SemaphoreType.DMA
    return pl.pallas_call(
        collect_kernel,
        out_shape=(
            jax.ShapeDtypeStruct((TOK, QUERY_HEADS * HEAD), BF16),
            jax.ShapeDtypeStruct((KV_HEADS, 2, TOK, HEAD), BF16),
            jax.ShapeDtypeStruct((8, HEAD), F32),
        ),
        in_specs=[any_, vmem, vmem],
        out_specs=(any_, any_, vmem),
        scratch_shapes=[
            pltpu.VMEM((2, 4, 2, TOK, HEAD), BF16),
            pltpu.VMEM((4, 2, TOK, HEAD), BF16),
            pltpu.VMEM((4, 2, TOK, HEAD), BF16),
            pltpu.VMEM((4, 2, TOK, HEAD), BF16),
            pltpu.VMEM((HALF, 8, HEAD), F32),
            pltpu.VMEM((8, 8, HEAD), F32),
            pltpu.VMEM((4, 8, HEAD), F32),
            pltpu.VMEM((8, HEAD), F32),
            pltpu.VMEM((8, HEAD), F32),
            dma((7,)), dma((HALF,)), dma((2,)), dma((2,)), dma, dma, dma((3,)), dma((4,)),
            dma((7,)), dma((HALF,)), dma((7,)), dma((8,)), dma((3,)), dma((4,)), dma((2,)),
        ],
        compiler_params=pltpu.CompilerParams(collective_id=1, has_side_effects=True, vmem_limit_bytes=24 << 20),
        name="collect",
    )(hq, hkv, curv)


def on_device(queries, keys_values, key_tangents, output_adjoint_rows, segments, span_pair):
    kv = jnp.concatenate([keys_values[0], key_tangents[0]], axis=1)
    kv = kv.reshape(TOK, 4, KV_HEADS, HEAD).transpose(2, 1, 0, 3)
    q, g, kv = spread(queries[0], output_adjoint_rows[0], kv)
    hq, hkv, curv = hvp(span_pair, segments.reshape(SHARDS, TOK), q, g, kv)
    hq, hkv, curv = collect(hq, hkv, curv)
    hkv = hkv.transpose(2, 1, 0, 3).reshape(1, TOK, 2, KV_HEADS * HEAD)
    return hq[None], hkv, curv[0, 0]


def solution(mesh):
    in_specs = (
        P("dp", "context", None),
        P("dp", "context", None, None),
        P("dp", "context", None, None),
        P("dp", "context", None),
        P("dp", None),
        P(),
    )
    out_specs = (P("dp", "context", None), P("dp", "context", None, None), P())
    return jax.shard_map(on_device, mesh=mesh, in_specs=in_specs, out_specs=out_specs, check_vma=False)
```

```python
import functools

import jax
import jax.numpy as jnp
from jax import lax
from jax.experimental import pallas as pl
from jax.experimental.pallas import tpu as pltpu
from jax.sharding import PartitionSpec as P

HEAD = 128
QUERY_HEADS = 32
KV_HEADS = 4
TOK = 128
SPAN = 64
WINDOW = 2048
SHARDS = 16
HALF = 8
OWN_HEADS = 4
OWN_COLS = OWN_HEADS * HEAD
ROWS = OWN_HEADS * SPAN
TILE = 256
TILES = WINDOW // TILE
BLOCKS = WINDOW // SPAN
CHUNKS = TILE // SPAN
SCALE = float(HEAD) ** -0.5
LOG2E = 1.4426950408889634
EXP_SCALE = SCALE * LOG2E
SAFE_LOG2 = 60.0
MESH = pl.DeviceIdType.MESH
F32 = jnp.float32
BF16 = jnp.bfloat16


def coordinates():
    dp = lax.axis_index("dp")
    context = lax.axis_index("context")
    return dp, context // HALF, (context // 2) % 4, context % 2


def context_index(z_hi, y, core):
    return z_hi * HALF + y * 2 + core


def remote(src, dst, send, recv, device):
    return pltpu.make_async_remote_copy(
        src_ref=src, dst_ref=dst, send_sem=send, recv_sem=recv, device_id=device, device_id_type=MESH
    )


def enter(devices):
    barrier = pltpu.get_barrier_semaphore()
    for device in devices:
        pl.semaphore_signal(barrier, inc=1, device_id=device, device_id_type=MESH)
    pl.semaphore_wait(barrier, len(devices))


def columns_of(y, core):
    return pl.ds(pl.multiple_of((y * 2 + core) * OWN_COLS, OWN_COLS), OWN_COLS)


def spread_kernel(q, g, kv, q_out, g_out, kv_out, kv_send, sib_send, z_send, zsib_send, q_send, g_send, kv_recv, q_recv, g_recv, local):
    dp, zh, y, c = coordinates()
    me = context_index(zh, y, c)
    sibling = (dp, context_index(zh, y, 1 - c))
    across = (dp, context_index(1 - zh, y, c))
    peers = []
    for dy in (1, 3, 2, 0):
        for dc in (0, 1):
            if dy or dc:
                peers.append(((y + dy) % 4, (c + dc) % 2))
    enter([(dp, context_index(zh, py, pc)) for py, pc in peers] + [across])

    own = zh * HALF + y * 2 + c
    slot_here = y * 2 + c
    locals_ = [
        pltpu.make_async_copy(kv.at[y], kv_out.at[own], local.at[0]),
        pltpu.make_async_copy(q.at[:, columns_of(y, c)], q_out.at[slot_here], local.at[1]),
        pltpu.make_async_copy(g.at[:, columns_of(y, c)], g_out.at[slot_here], local.at[2]),
    ]
    copies = []

    def start(copy):
        copy.start()
        copies.append(copy)

    for n, dy in enumerate((1, 3, 2)):
        ty = (y + dy) % 4
        start(remote(kv.at[ty], kv_out.at[own], kv_send.at[n], kv_recv.at[own], (dp, context_index(zh, ty, c))))
    start(remote(kv.at[y], kv_out.at[own], z_send.at[0], kv_recv.at[own], across))
    start(remote(kv.at[y], kv_out.at[own], sib_send.at[0], kv_recv.at[own], sibling))
    for copy in locals_:
        copy.start()
    for n, dy in enumerate((1, 3, 2)):
        slot = context_index(zh, (y + 4 - dy) % 4, c)
        here = kv_out.at[slot]
        remote(here, here, kv_send.at[n], kv_recv.at[slot], across).wait_recv()
        start(remote(here, here, z_send.at[1 + n], kv_recv.at[slot], across))
        start(remote(here, here, sib_send.at[1 + n], kv_recv.at[slot], sibling))
    for n, (py, pc) in enumerate(peers):
        target = (dp, context_index(zh, py, pc))
        start(remote(q.at[:, columns_of(py, pc)], q_out.at[slot_here], q_send.at[n], q_recv.at[slot_here], target))
        start(remote(g.at[:, columns_of(py, pc)], g_out.at[slot_here], g_send.at[n], g_recv.at[slot_here], target))
    for n, dy in enumerate((0, 1, 3, 2)):
        slot = context_index(1 - zh, (y + 4 - dy) % 4, c)
        here = kv_out.at[slot]
        remote(here, here, z_send.at[n], kv_recv.at[slot], across).wait_recv()
        start(remote(here, here, zsib_send.at[n], kv_recv.at[slot], sibling))
    for z in range(2):
        for ys in range(4):
            slot = context_index(z, ys, 1 - c)
            here = kv_out.at[slot]
            remote(here, here, z_send.at[0], kv_recv.at[slot], sibling).wait_recv()
    for n, (py, pc) in enumerate(peers):
        slot = py * 2 + pc
        remote(q_out.at[slot], q_out.at[slot], q_send.at[n], q_recv.at[slot], sibling).wait_recv()
        remote(g_out.at[slot], g_out.at[slot], g_send.at[n], g_recv.at[slot], sibling).wait_recv()
    for copy in copies:
        copy.wait_send()
    for copy in locals_:
        copy.wait()


def spread(q, g, kv):
    any_ = pl.BlockSpec(memory_space=pl.ANY)
    dma = pltpu.SemaphoreType.DMA
    return pl.pallas_call(
        spread_kernel,
        out_shape=(
            jax.ShapeDtypeStruct((HALF, TOK, OWN_COLS), BF16),
            jax.ShapeDtypeStruct((HALF, TOK, OWN_COLS), BF16),
            jax.ShapeDtypeStruct((SHARDS, 4, TOK, HEAD), BF16),
        ),
        in_specs=[any_] * 3,
        out_specs=(any_,) * 3,
        scratch_shapes=[
            dma((3,)), dma((4,)), dma((4,)), dma((4,)), dma((7,)), dma((7,)),
            dma((SHARDS,)), dma((HALF,)), dma((HALF,)), dma((3,)),
        ],
        compiler_params=pltpu.CompilerParams(collective_id=0, has_side_effects=True),
        name="spread",
    )(q, g, kv)


def nt_dot(a, b):
    return lax.dot_general(a, b, (((1,), (1,)), ((), ())), preferred_element_type=F32)


def nn_dot(a, b):
    return jnp.dot(a, b, preferred_element_type=F32)


def fold_rows(x):
    return jnp.sum(x.reshape(x.shape[0] // 8, 8, x.shape[1]), axis=0)


def hvp_kernel(pair, seg, q, g, kv, hq_out, hkv_out, curv_out, kt, vt, k_t, tk_t, qt, gt, q_rows, g_rows, even, odd, p_even, p_odd, hk_acc, hv_acc, hq_acc):
    _, zh, _, _ = coordinates()
    segments = seg[...]
    starts = [jnp.sum((segments < d).astype(jnp.int32)) for d in (1, 2, 3)]

    ones = jnp.ones((HEAD, HEAD), BF16)

    def fold_max(x):
        return jnp.max(x.reshape(x.shape[0] // 8, 8, x.shape[1]), axis=0)

    def split_into(row, x):
        high = x.astype(BF16)
        kt[pl.ds(row, SPAN), 0:HEAD] = high
        kt[pl.ds(row, SPAN), HEAD:] = (x - high.astype(F32)).astype(BF16)

    def key_place(block):
        tile = block // CHUNKS
        return pl.multiple_of(tile * (2 * TILE) + (block % CHUNKS) * SPAN, SPAN)

    def prepare(i, carry):
        first = pair[i]
        for half in range(2):
            block = first if half == 0 else BLOCKS - 1 - first
            row = key_place(block)
            rows = pl.ds(half * SPAN, SPAN)
            k = kv[i, 0, rows, :].astype(F32)
            tk = kv[i, 2, rows, :].astype(F32)
            split_into(row, k * EXP_SCALE)
            split_into(row + TILE, tk * SCALE)
            vt[pl.ds(row, SPAN), :] = kv[i, 1, rows, :]
            vt[pl.ds(row + TILE, SPAN), :] = kv[i, 3, rows, :]
            here = pl.ds(pl.multiple_of(block * SPAN, SPAN), SPAN)
            hk_acc[here, :] = k
            hv_acc[here, :] = tk
            carry = jnp.maximum(carry, fold_max(nn_dot((k * k).astype(BF16), ones)))
        return carry

    key_norm = lax.fori_loop(0, SHARDS, prepare, jnp.zeros((8, HEAD), F32))

    def turn(t, carry):
        here = pl.ds(pl.multiple_of(t * TILE, TILE), TILE)
        k_t[:, here] = hk_acc[here, :].T.astype(BF16)
        tk_t[:, here] = hv_acc[here, :].T.astype(BF16)
        hk_acc[here, :] = jnp.zeros((TILE, HEAD), F32)
        hv_acc[here, :] = jnp.zeros((TILE, HEAD), F32)
        return carry

    lax.fori_loop(0, TILES, turn, 0)

    def query_norms(s, carry):
        for h in range(OWN_HEADS):
            x = q[s, :, h * HEAD:(h + 1) * HEAD].astype(F32)
            carry = jnp.maximum(carry, fold_max(nn_dot((x * x).astype(BF16), ones)))
        return carry

    query_norm = lax.fori_loop(0, HALF, query_norms, jnp.zeros((8, HEAD), F32))
    bound = jnp.max(key_norm) * jnp.max(query_norm) * (EXP_SCALE * EXP_SCALE)
    safe = bound < SAFE_LOG2 * SAFE_LOG2

    lane = lax.broadcasted_iota(jnp.int32, (1, ROWS), 1)
    key_row = lax.broadcasted_iota(jnp.int32, (SPAN, ROWS), 0)

    def query_block(n, carry):
        s = n // 2
        half = n % 2
        first = pair[zh * HALF + s]
        block = jnp.where(half == 0, first, BLOCKS - 1 - first)
        base = block * SPAN
        rows = pl.ds(pl.multiple_of(half * SPAN, SPAN), SPAN)
        for h in range(OWN_HEADS):
            cols = slice(h * HEAD, (h + 1) * HEAD)
            part = slice(h * SPAN, (h + 1) * SPAN)
            q_rows[part, :] = q[s, rows, cols]
            g_rows[part, :] = g[s, rows, cols]
        qt_half = q_rows[...].astype(F32).T.astype(BF16)
        qt[0:HEAD, :] = qt_half
        qt[HEAD:, :] = qt_half
        gt[...] = g_rows[...].astype(F32).T.astype(BF16)
        query_pos = base + lane % SPAN
        doc_start = jnp.zeros_like(query_pos)
        low = jnp.int32(0)
        for start in starts:
            doc_start = jnp.where(query_pos >= start, start, doc_start)
            low = jnp.where(base >= start, start, low)
        first_tile = low // TILE
        tiles = base // TILE + 1 - first_tile
        pairs = (tiles - 1) // 2
        oldest = doc_start - first_tile * TILE
        newest = query_pos - first_tile * TILE

        def seen_in(r, c):
            key_pos = r * TILE + c * SPAN + key_row
            return (key_pos >= oldest) & (key_pos <= newest)

        def key_rows(t):
            return pl.ds(pl.multiple_of(t * (2 * TILE), 2 * TILE), 2 * TILE)

        def peak_pass(_):
            def step(r, top):
                st = nn_dot(kt[key_rows(first_tile + r), :], qt[...])
                for c in range(CHUNKS):
                    masked = jnp.where(seen_in(r, c), st[c * SPAN:(c + 1) * SPAN], -1e30)
                    top = jnp.maximum(top, fold_max(masked))
                return top
            top = lax.fori_loop(0, tiles, step, jnp.full((8, ROWS), -1e30, F32))
            return jnp.max(top, axis=0, keepdims=True)

        peak = lax.cond(safe, lambda _: jnp.zeros((1, ROWS), F32), peak_pass, 0)

        def multiply(r, store):
            where = key_rows(first_tile + r)
            store[r // 2, 0] = nn_dot(kt[where, :], qt[...])
            store[r // 2, 1] = nn_dot(vt[where, :], gt[...])

        def tally(r, store, carry):
            total, mu, delta, mixed = carry
            for c in range(CHUNKS):
                a = slice(c * SPAN, (c + 1) * SPAN)
                b = slice(TILE + c * SPAN, TILE + (c + 1) * SPAN)
                w = jnp.where(seen_in(r, c), jnp.exp2(store[r // 2, 0, a] - peak), 0.0)
                store[r // 2, 0, a] = w
                ts = store[r // 2, 0, b]
                dprob = store[r // 2, 1, a]
                total = total + fold_rows(w)
                mu = mu + fold_rows(w * ts)
                delta = delta + fold_rows(w * dprob)
                mixed = mixed + fold_rows(w * (ts * dprob + store[r // 2, 1, b]))
            return total, mu, delta, mixed

        def stats_pair(u, carry):
            multiply(2 * u + 1, odd)
            carry = tally(2 * u, even, carry)
            multiply(2 * u + 2, even)
            return tally(2 * u + 1, odd, carry)

        def stats_two(carry):
            multiply(tiles - 1, odd)
            return tally(tiles - 1, odd, tally(tiles - 2, even, carry))

        zero = jnp.zeros((8, ROWS), F32)
        multiply(0, even)
        sums = lax.fori_loop(0, pairs, stats_pair, (zero,) * 4)
        one_left = tiles % 2 == 1
        sums = lax.cond(one_left, functools.partial(tally, tiles - 1, even), stats_two, sums)
        total, mu, delta, mixed = [jnp.sum(x, axis=0, keepdims=True) for x in sums]
        inverse = 1.0 / total
        mu = mu * inverse
        delta = delta * inverse
        tdelta = mixed * inverse - mu * delta

        hq_acc[...] = jnp.zeros_like(hq_acc)

        def weigh(r, store, ready):
            for c in range(CHUNKS):
                a = slice(c * SPAN, (c + 1) * SPAN)
                b = slice(TILE + c * SPAN, TILE + (c + 1) * SPAN)
                prob = store[r // 2, 0, a] * inverse
                tsc = store[r // 2, 0, b] - mu
                dpc = store[r // 2, 1, a] - delta
                tdc = store[r // 2, 1, b] - tdelta
                ready[a, :] = (prob * (tsc * dpc + tdc)).astype(BF16)
                ready[b, :] = (prob * dpc).astype(BF16)
                ready[2 * TILE + c * SPAN:2 * TILE + (c + 1) * SPAN, :] = (prob * tsc).astype(BF16)

        def add(r, ready):
            here = pl.ds(pl.multiple_of((first_tile + r) * TILE, TILE), TILE)
            hk_acc[here, :] += nn_dot(ready[0:TILE], q_rows[...])
            hv_acc[here, :] += nn_dot(ready[2 * TILE:], g_rows[...])
            keys = jnp.concatenate([k_t[:, here], tk_t[:, here]], axis=1)
            hq_acc[...] += nn_dot(keys, ready[0:2 * TILE])

        def grads_pair(u, carry):
            weigh(2 * u + 1, odd, p_odd)
            add(2 * u, p_even)
            weigh(2 * u + 2, even, p_even)
            add(2 * u + 1, p_odd)
            return carry

        def grads_two():
            weigh(tiles - 1, odd, p_odd)
            add(tiles - 2, p_even)
            add(tiles - 1, p_odd)

        weigh(0, even, p_even)
        lax.fori_loop(0, pairs, grads_pair, 0)
        pl.when(one_left)(lambda: add(tiles - 1, p_even))
        pl.when(jnp.logical_not(one_left))(grads_two)
        hq = (hq_acc[...] * SCALE).T.astype(BF16)
        for h in range(OWN_HEADS):
            hq_out[s, rows, h * HEAD:(h + 1) * HEAD] = hq[h * SPAN:(h + 1) * SPAN]
        return carry

    lax.fori_loop(0, 2 * HALF, query_block, 0)

    def finish(i, carry):
        first = pair[i]
        for half in range(2):
            block = first if half == 0 else BLOCKS - 1 - first
            here = pl.ds(pl.multiple_of(block * SPAN, SPAN), SPAN)
            rows = pl.ds(half * SPAN, SPAN)
            hk = hk_acc[here, :] * SCALE
            hv = hv_acc[here, :]
            carry = carry + fold_rows(kv[i, 2, rows, :].astype(F32) * hk)
            carry = carry + fold_rows(kv[i, 3, rows, :].astype(F32) * hv)
            z = i // HALF
            ys = (i // 2) % 4
            core = i % 2
            hkv_out[core, z, ys, 0, rows, :] = hk.astype(BF16)
            hkv_out[core, z, ys, 1, rows, :] = hv.astype(BF16)
        return carry

    curv = lax.fori_loop(0, SHARDS, finish, jnp.zeros((8, HEAD), F32))
    curv_out[...] = jnp.full((8, HEAD), jnp.sum(curv), F32)


def hvp(pair, seg, q, g, kv):
    vmem = pl.BlockSpec(memory_space=pltpu.VMEM)
    return pl.pallas_call(
        hvp_kernel,
        out_shape=(
            jax.ShapeDtypeStruct((HALF, TOK, OWN_COLS), BF16),
            jax.ShapeDtypeStruct((2, 2, 4, 2, TOK, HEAD), BF16),
            jax.ShapeDtypeStruct((8, HEAD), F32),
        ),
        in_specs=[pl.BlockSpec(memory_space=pltpu.SMEM)] + [vmem] * 4,
        out_specs=(vmem,) * 3,
        scratch_shapes=[
            pltpu.VMEM((2 * WINDOW, 2 * HEAD), BF16),
            pltpu.VMEM((2 * WINDOW, HEAD), BF16),
            pltpu.VMEM((HEAD, WINDOW), BF16),
            pltpu.VMEM((HEAD, WINDOW), BF16),
            pltpu.VMEM((2 * HEAD, ROWS), BF16),
            pltpu.VMEM((HEAD, ROWS), BF16),
            pltpu.VMEM((ROWS, HEAD), BF16),
            pltpu.VMEM((ROWS, HEAD), BF16),
            pltpu.VMEM(((TILES + 1) // 2, 2, 2 * TILE, ROWS), F32),
            pltpu.VMEM(((TILES + 1) // 2, 2, 2 * TILE, ROWS), F32),
            pltpu.VMEM((3 * TILE, ROWS), BF16),
            pltpu.VMEM((3 * TILE, ROWS), BF16),
            pltpu.VMEM((WINDOW, HEAD), F32),
            pltpu.VMEM((WINDOW, HEAD), F32),
            pltpu.VMEM((HEAD, ROWS), F32),
        ],
        compiler_params=pltpu.CompilerParams(vmem_limit_bytes=50 << 20),
        name="hvp",
    )(pair, seg, q, g, kv)


def collect_kernel(hq, hkv, curv, hq_out, hkv_out, curv_out, sib_buf, z_buf, z_stage, y_stage, a_buf, b_buf, c_buf, b_own, c_own, hq_send, hq_recv, sib_send, sib_recv, z_send, z_recv, y_send, y_recv, a_send, a_recv, b_send, b_recv, c_send, c_recv, local):
    dp, zh, y, c = coordinates()
    x = dp % 4
    z_lo = dp // 4
    z = zh * 4 + z_lo
    sibling = (dp, context_index(zh, y, 1 - c))
    across = (dp, context_index(1 - zh, y, c))
    peers = []
    for dy in (1, 3, 2, 0):
        for dc in (0, 1):
            if dy or dc:
                peers.append(((y + dy) % 4, (c + dc) % 2))
    row_devices = [(dp, context_index(zh, py, pc)) for py, pc in peers]
    z_peers = [(z + dz) % 8 for dz in range(1, 8)]
    z_devices = [((pz % 4) * 4 + x, context_index(pz // 4, y, c)) for pz in z_peers]
    x_peers = [(x + dx) % 4 for dx in range(1, 4)]
    x_devices = [(z_lo * 4 + px, context_index(zh, y, c)) for px in x_peers]
    enter(row_devices + z_devices + x_devices)

    copies = []

    def start(copy):
        copy.start()
        copies.append(copy)

    slot_here = y * 2 + c
    for n, which in enumerate((1 - zh, zh)):
        start(remote(hkv.at[1 - c, which], sib_buf.at[which], sib_send.at[n], sib_recv.at[n], sibling))
    for n, device in enumerate(row_devices):
        start(remote(curv, a_buf.at[slot_here], a_send.at[n], a_recv.at[slot_here], device))
    for n, (py, pc) in enumerate(peers):
        start(remote(hq.at[py * 2 + pc], hq_out.at[:, columns_of(y, c)], hq_send.at[n], hq_recv.at[slot_here], row_devices[n]))
    own_hq = pltpu.make_async_copy(hq.at[slot_here], hq_out.at[:, columns_of(y, c)], local.at[0])
    own_hq.start()

    other = 1 - zh
    remote(sib_buf.at[other], sib_buf.at[other], sib_send.at[0], sib_recv.at[0], sibling).wait_recv()
    for ys in range(4):
        for part in range(2):
            z_stage[ys, part] = (hkv[c, other, ys, part].astype(F32) + sib_buf[other, ys, part].astype(F32)).astype(BF16)
    start(remote(z_stage, z_buf, z_send, z_recv, across))

    for n, (py, pc) in enumerate(peers):
        slot = py * 2 + pc
        remote(a_buf.at[slot], a_buf.at[slot], a_send.at[n], a_recv.at[slot], sibling).wait_recv()
    a_buf[slot_here] = curv[...]
    b_own[...] = jnp.sum(a_buf[...], axis=0)
    for n, device in enumerate(z_devices):
        start(remote(b_own, b_buf.at[z], b_send.at[n], b_recv.at[z], device))
    for n, pz in enumerate(z_peers):
        remote(b_buf.at[pz], b_buf.at[pz], b_send.at[n], b_recv.at[pz], sibling).wait_recv()
    b_buf[z] = b_own[...]
    c_own[...] = jnp.sum(b_buf[...], axis=0)
    for n, device in enumerate(x_devices):
        start(remote(c_own, c_buf.at[x], c_send.at[n], c_recv.at[x], device))
    for n, px in enumerate(x_peers):
        remote(c_buf.at[px], c_buf.at[px], c_send.at[n], c_recv.at[px], sibling).wait_recv()
    c_buf[x] = c_own[...]
    curv_out[...] = jnp.sum(c_buf[...], axis=0) * (1.0 / (SHARDS * WINDOW))

    remote(sib_buf.at[zh], sib_buf.at[zh], sib_send.at[1], sib_recv.at[1], sibling).wait_recv()
    remote(z_stage, z_buf, z_send, z_recv, across).wait_recv()
    for ys in range(4):
        for part in range(2):
            total = hkv[c, zh, ys, part].astype(F32) + sib_buf[zh, ys, part].astype(F32) + z_buf[ys, part].astype(F32)
            y_stage[ys, part] = total.astype(BF16)
    for n, dy in enumerate((1, 3, 2)):
        ty = (y + dy) % 4
        start(remote(y_stage.at[ty], hkv_out.at[y], y_send.at[n], y_recv.at[y], (dp, context_index(zh, ty, c))))
    own_kv = pltpu.make_async_copy(y_stage.at[y], hkv_out.at[y], local.at[1])
    own_kv.start()
    for n, dy in enumerate((1, 3, 2)):
        ty = (y + dy) % 4
        remote(hkv_out.at[ty], hkv_out.at[ty], y_send.at[n], y_recv.at[ty], sibling).wait_recv()
    for n, (py, pc) in enumerate(peers):
        slot = py * 2 + pc
        remote(hq.at[slot], hq_out.at[:, columns_of(py, pc)], hq_send.at[n], hq_recv.at[slot], sibling).wait_recv()
    for copy in copies:
        copy.wait_send()
    own_hq.wait()
    own_kv.wait()


def collect(hq, hkv, curv):
    vmem = pl.BlockSpec(memory_space=pltpu.VMEM)
    any_ = pl.BlockSpec(memory_space=pl.ANY)
    dma = pltpu.SemaphoreType.DMA
    return pl.pallas_call(
        collect_kernel,
        out_shape=(
            jax.ShapeDtypeStruct((TOK, QUERY_HEADS * HEAD), BF16),
            jax.ShapeDtypeStruct((KV_HEADS, 2, TOK, HEAD), BF16),
            jax.ShapeDtypeStruct((8, HEAD), F32),
        ),
        in_specs=[any_, vmem, vmem],
        out_specs=(any_, any_, vmem),
        scratch_shapes=[
            pltpu.VMEM((2, 4, 2, TOK, HEAD), BF16),
            pltpu.VMEM((4, 2, TOK, HEAD), BF16),
            pltpu.VMEM((4, 2, TOK, HEAD), BF16),
            pltpu.VMEM((4, 2, TOK, HEAD), BF16),
            pltpu.VMEM((HALF, 8, HEAD), F32),
            pltpu.VMEM((8, 8, HEAD), F32),
            pltpu.VMEM((4, 8, HEAD), F32),
            pltpu.VMEM((8, HEAD), F32),
            pltpu.VMEM((8, HEAD), F32),
            dma((7,)), dma((HALF,)), dma((2,)), dma((2,)), dma, dma, dma((3,)), dma((4,)),
            dma((7,)), dma((HALF,)), dma((7,)), dma((8,)), dma((3,)), dma((4,)), dma((2,)),
        ],
        compiler_params=pltpu.CompilerParams(collective_id=1, has_side_effects=True, vmem_limit_bytes=24 << 20),
        name="collect",
    )(hq, hkv, curv)


def on_device(queries, keys_values, key_tangents, output_adjoint_rows, segments, span_pair):
    kv = jnp.concatenate([keys_values[0], key_tangents[0]], axis=1)
    kv = kv.reshape(TOK, 4, KV_HEADS, HEAD).transpose(2, 1, 0, 3)
    q, g, kv = spread(queries[0], output_adjoint_rows[0], kv)
    hq, hkv, curv = hvp(span_pair, segments.reshape(SHARDS, TOK), q, g, kv)
    hq, hkv, curv = collect(hq, hkv, curv)
    hkv = hkv.transpose(2, 1, 0, 3).reshape(1, TOK, 2, KV_HEADS * HEAD)
    return hq[None], hkv, curv[0, 0]


def solution(mesh):
    in_specs = (
        P("dp", "context", None),
        P("dp", "context", None, None),
        P("dp", "context", None, None),
        P("dp", "context", None),
        P("dp", None),
        P(),
    )
    out_specs = (P("dp", "context", None), P("dp", "context", None, None), P())
    return jax.shard_map(on_device, mesh=mesh, in_specs=in_specs, out_specs=out_specs, check_vma=False)
```
